32 devices in a mesh: dp: 2 (over x), seq: 16 (over z, y, core).
Axes of the slice: x: 2, y: 2, z: 4, core: 2. Of those that a mesh axis runs over, the one named last changes fastest.
Arguments:
- inputs: bfloat16 [2, 16384, 1024], P('dp', 'seq'), may hold values from -6 to 6
- cotangent: bfloat16 [2, 16384, 1024], P('dp', 'seq'), may hold values from -4 to 4
- factor_one: bfloat16 [16, 1024, 1024], P('seq'), may hold values from -0.1875 to 0.1875
- factor_two: bfloat16 [16, 1024, 1024], P('seq'), may hold values from -0.1875 to 0.1875
Outputs:
- mixed: bfloat16 [2, 16384, 1024], P('dp', 'seq')
- grad_input: bfloat16 [2, 16384, 1024], P('dp', 'seq')
- grad_one: float32 [16, 1024, 1024], P('seq', 'dp')
- grad_two: float32 [16, 1024, 1024], P('seq', 'dp')
The draws below stay inside these ranges and needn't reach their ends.
All inputs are finite; a program needn't handle non-finite values.
Results may differ from the reference program's by a relative error of at most 0.014.
Values may be sent and summed in bfloat16 or wider, within the bound.
A program may use at most 128 MiB of HBM per device.

```python
import jax
import jax.numpy as jnp
from jax import lax

D = 1024
BLK = 1024
SEQS_DEV = 1
BATCH = 2
NBLK = 16
L = 16384
N_DP = 2


def levels(stream_key, dims, split, smallest, high):
    def one(position, blocks):
        draws = jax.random.uniform(jax.random.fold_in(jax.random.fold_in(stream_key, 6), position), (blocks,), jnp.float32, smallest / len(split), high / len(split))
        return jnp.repeat(jnp.exp(draws), dims[position] // blocks).reshape((-1,) + (1,) * (len(dims) - position - 1))

    level = one(*split[0])
    for cut in split[1:]:
        level = level * one(*cut)
    return level


def noise(key, dims, deviation, limit, shards=(), dtype=jnp.bfloat16):
    result = deviation * jax.random.normal(key, dims, jnp.float32)
    if shards:
        result = result * levels(key, dims, shards, -0.22, 0.18)
    return jnp.clip(result, -limit, limit).astype(dtype)


def setup_inputs(seed: int = 0) -> dict:
    key_of = jax.random.split(jax.random.key(seed), 5)
    inputs = noise(key_of[0], (BATCH, L, D), 1.0, 6.0, ((0, 2), (1, 16)))
    cotangent = noise(key_of[1], (BATCH, L, D), 0.5, 4.0, ((0, 2), (1, 16)))
    factor_one = noise(key_of[2], (NBLK, BLK, BLK), BLK ** -0.5, 0.1875, ((0, 16),))
    factor_two = noise(key_of[3], (NBLK, BLK, BLK), BLK ** -0.5, 0.1875, ((0, 16),))
    return {"inputs": inputs, "cotangent": cotangent, "factor_one": factor_one, "factor_two": factor_two}


def to_moved(data):
    seqs = data.shape[0]
    parts = data.reshape(seqs, NBLK, NBLK, BLK // NBLK, D)
    return jnp.transpose(parts, (0, 2, 3, 1, 4)).reshape(seqs, NBLK, BLK, D)


def from_moved(data):
    seqs = data.shape[0]
    parts = data.reshape(seqs, NBLK, BLK // NBLK, NBLK, D)
    return jnp.transpose(parts, (0, 3, 1, 2, 4)).reshape(seqs, NBLK, BLK, D)


def one_group(inputs, cotangent, factor_one, factor_two):
    seqs = inputs.shape[0]
    xb = inputs.reshape(seqs, NBLK, BLK, D)
    dyb = cotangent.reshape(seqs, NBLK, BLK, D)
    fone = factor_one.astype(jnp.float32)
    ftwo = factor_two.astype(jnp.float32)
    first = jnp.einsum("mkj,smjc->smkc", fone, xb.astype(jnp.float32)).astype(jnp.bfloat16)
    moved = to_moved(first)
    second = jnp.einsum("jpq,sjqc->sjpc", ftwo, moved.astype(jnp.float32)).astype(jnp.bfloat16)
    monarch = from_moved(second)
    mixed = (xb.astype(jnp.float32) * monarch.astype(jnp.float32)).astype(jnp.bfloat16)
    gated = (dyb.astype(jnp.float32) * xb.astype(jnp.float32)).astype(jnp.bfloat16)
    gated_moved = to_moved(gated)
    part_two = jnp.einsum("sjpc,sjqc->jpq", gated_moved.astype(jnp.float32), moved.astype(jnp.float32))
    back_two = jnp.einsum("jpq,sjpc->sjqc", ftwo, gated_moved.astype(jnp.float32)).astype(jnp.bfloat16)
    back_moved = from_moved(back_two)
    part_one = jnp.einsum("smkc,smjc->mkj", back_moved.astype(jnp.float32), xb.astype(jnp.float32))
    grad_input = dyb.astype(jnp.float32) * monarch.astype(jnp.float32)
    grad_input = grad_input + jnp.einsum("mkj,smkc->smjc", fone, back_moved.astype(jnp.float32))
    return (mixed.reshape(seqs, L, D), grad_input.astype(jnp.bfloat16).reshape(seqs, L, D),
            part_one.astype(jnp.bfloat16), part_two.astype(jnp.bfloat16))


def reference(inputs, cotangent, factor_one, factor_two):
    xs = inputs.reshape(N_DP, SEQS_DEV, L, D)
    dys = cotangent.reshape(N_DP, SEQS_DEV, L, D)

    def step(carry, pair):
        mixed, grad_input, part_one, part_two = one_group(pair[0], pair[1], factor_one, factor_two)
        total_one = carry[0] + part_one.astype(jnp.float32)
        total_two = carry[1] + part_two.astype(jnp.float32)
        return (total_one, total_two), (mixed, grad_input)

    start = (jnp.zeros((NBLK, BLK, BLK), jnp.float32), jnp.zeros((NBLK, BLK, BLK), jnp.float32))
    totals, outs = lax.scan(step, start, (xs, dys))
    mixed = outs[0].reshape(BATCH, L, D)
    grad_input = outs[1].reshape(BATCH, L, D)
    return (mixed, grad_input, totals[0], totals[1])
```

```python
import functools

import jax
import jax.numpy as jnp
from jax import lax
from jax.experimental import pallas as pl
from jax.experimental.pallas import tpu as pltpu
from jax.sharding import PartitionSpec as P

MESH = pl.DeviceIdType.MESH
F32 = jnp.float32
BF16 = jnp.bfloat16

CHUNKS = 4
TILE = 256
DEPTH = 3

GATED, FIRST, BACK, SECOND = range(4)


def nn(a, b):
    return jnp.dot(a, b, preferred_element_type=F32)


def nt(a, b):
    return lax.dot_general(a, b, (((1,), (1,)), ((), ())), preferred_element_type=F32)


def loop(n, body):
    def step(i, carry):
        body(i)
        return carry

    lax.fori_loop(0, n, step, 0)


def kernel(
    count,
    ndp,
    x_hbm,
    c_hbm,
    f1_hbm,
    f2_hbm,
    mixed_hbm,
    gin_hbm,
    g1_hbm,
    g2_hbm,
    xv,
    cv,
    f1,
    f1t,
    f2,
    f2p,
    f2pt,
    tmp,
    send0,
    send1,
    send2,
    send3,
    recv0,
    recv1,
    recv2,
    recv3,
    spread,
    p1,
    p2,
    r1,
    r2,
    g1,
    g2,
    ssem,
    rsem,
    dssem,
    drsem,
    insem,
    outsem,
):
    sends = (send0, send1, send2, send3)
    recvs = (recv0, recv1, recv2, recv3)
    parts = (p1, p2)
    others = (r1, r2)
    chunks, block, width = xv.shape
    tiles = block // TILE
    rows = block // count
    piece = block // ndp
    dp = lax.axis_index("dp")
    me = lax.axis_index("seq")

    def rowsof(t):
        return pl.ds(pl.multiple_of(t * TILE, TILE), TILE)

    def load(src, dst, i):
        return pltpu.make_async_copy(src, dst, insem.at[i])

    loads = []
    for n in range(chunks):
        cols = pl.ds(n * width, width)
        loads.append(load(x_hbm.at[:, cols], xv.at[n], 2 * n))
        loads.append(load(c_hbm.at[:, cols], cv.at[n], 2 * n + 1))
    load_f1 = load(f1_hbm, f1, 2 * chunks)
    load_f2 = load(f2_hbm, f2, 2 * chunks + 1)
    for copy in loads:
        copy.start()
    load_f1.start()
    load_f2.start()

    barrier = pltpu.get_barrier_semaphore()

    def greet_seq(i):
        pl.semaphore_signal(
            barrier, inc=1, device_id=(dp, (me + 1 + i) % count), device_id_type=MESH
        )

    def greet_dp(i):
        pl.semaphore_signal(
            barrier, inc=1, device_id=((dp + 1 + i) % ndp, me), device_id_type=MESH
        )

    loop(count - 1, greet_seq)
    loop(ndp - 1, greet_dp)

    def seq_copy(t, n, source, target, size, to):
        return pltpu.make_async_remote_copy(
            src_ref=sends[t].at[n, pl.ds(source, size)],
            dst_ref=recvs[t].at[n, pl.ds(target, size)],
            send_sem=ssem.at[t, n],
            recv_sem=rsem.at[t, n],
            device_id=(dp, to),
            device_id_type=MESH,
        )

    mine = pl.multiple_of(me * rows, rows)

    def send(t, n):
        def one(i):
            offset = count // 2 + ((i + 1) // 2) * (1 - 2 * (i % 2))
            to = (me + offset) % count
            seq_copy(t, n, pl.multiple_of(to * rows, rows), mine, rows, to).start()

        loop(count - 1, one)
        recvs[t][n, pl.ds(mine, rows), :] = sends[t][n, pl.ds(mine, rows), :]

    def whole(t, n):
        return seq_copy(t, n, 0, 0, (count - 1) * rows, (me + 1) % count)

    def dp_copy(g, source, target, size, to):
        return pltpu.make_async_remote_copy(
            src_ref=parts[g].at[pl.ds(source, size)],
            dst_ref=others[g].at[pl.ds(target, size)],
            send_sem=dssem.at[g],
            recv_sem=drsem.at[g],
            device_id=(to, me),
            device_id_type=MESH,
        )

    own = pl.multiple_of(dp * piece, piece)

    def dp_send(g):
        def one(i):
            to = (dp + 1 + i) % ndp
            dp_copy(g, pl.multiple_of(to * piece, piece), own, piece, to).start()

        loop(ndp - 1, one)

    def dp_whole(g):
        return dp_copy(g, 0, 0, (ndp - 1) * piece, (dp + 1) % ndp)

    def dp_finish(g, out, out_hbm):
        dp_whole(g).wait_recv()
        others[g][pl.ds(own, piece), :] = parts[g][pl.ds(own, piece), :]
        step = min(piece, 128)

        def add(i):
            total = others[g][pl.ds(pl.multiple_of(i * step, step), step), :].astype(F32)
            for d in range(1, ndp):
                at = pl.multiple_of(d * piece + i * step, step)
                total += others[g][pl.ds(at, step), :].astype(F32)
            out[pl.ds(pl.multiple_of(i * step, step), step), :] = total

        loop(piece // step, add)
        copy = pltpu.make_async_copy(out, out_hbm, outsem.at[2 * chunks + g])
        copy.start()
        return copy

    shift = count.bit_length() - 1
    back_shift = rows.bit_length() - 1

    def select(t, forth):
        row = lax.broadcasted_iota(jnp.int32, (TILE, block), 0) + t * TILE
        col = lax.broadcasted_iota(jnp.int32, (TILE, block), 1)
        if forth:
            want = (row & (rows - 1)) * count + lax.shift_right_logical(
                row, jnp.full_like(row, back_shift)
            )
        else:
            want = (row & (count - 1)) * rows + lax.shift_right_logical(
                row, jnp.full_like(row, shift)
            )
        return jnp.where(col == want, 1.0, 0.0).astype(BF16)

    def identity(t):
        row = lax.broadcasted_iota(jnp.int32, (TILE, block), 0) + t * TILE
        col = lax.broadcasted_iota(jnp.int32, (TILE, block), 1)
        return jnp.where(col == row, 1.0, 0.0).astype(BF16)

    def make_gated(n):
        def tile(t):
            s = rowsof(t)
            send0[n, s, :] = (cv[n, s, :].astype(F32) * xv[n, s, :].astype(F32)).astype(BF16)

        loop(tiles, tile)

    def make_product(left, right, out, n):
        def tile(t):
            s = rowsof(t)
            out[n, s, :] = nn(left[s, :], right[n]).astype(out.dtype)

        loop(tiles, tile)

    def arrange_factors():
        def flip(t):
            f1t[rowsof(t), :] = nt(identity(t), f1[...]).astype(BF16)

        loop(tiles, flip)

        load_f2.wait()

        def one(t):
            tmp[rowsof(t), :] = nn(select(t, True), f2[...]).astype(BF16)

        def two(t):
            f2pt[rowsof(t), :] = nt(select(t, True), tmp[...]).astype(BF16)

        def three(t):
            tmp[rowsof(t), :] = nt(select(t, True), f2[...]).astype(BF16)

        def four(t):
            f2p[rowsof(t), :] = nt(select(t, True), tmp[...]).astype(BF16)

        loop(tiles, one)
        loop(tiles, two)
        loop(tiles, three)
        loop(tiles, four)

    def grad_two_part():
        def outer(t):
            s = rowsof(t)
            total = nt(recv0[0, s, :], recv1[0])
            for n in range(1, chunks):
                total += nt(recv0[n, s, :], recv1[n])
            p2[s, :] = total.astype(BF16)

        def one(t):
            tmp[rowsof(t), :] = nt(select(t, False), p2[...]).astype(BF16)

        def two(t):
            p2[rowsof(t), :] = nt(select(t, False), tmp[...]).astype(BF16)

        loop(tiles, outer)
        loop(tiles, one)
        loop(tiles, two)

    def grad_one_part():
        def outer(t):
            s = rowsof(t)
            total = nt(recv2[0, s, :], xv[0])
            for n in range(1, chunks):
                total += nt(recv2[n, s, :], xv[n])
            p1[s, :] = total.astype(BF16)

        loop(tiles, outer)

    half = chunks // 2
    units = [(GATED, n) for n in range(chunks)]
    units += [(FIRST, n) for n in range(half)]
    units += [(BACK, n) for n in range(chunks)]
    units += [(FIRST, n) for n in range(half, chunks)]
    units += [(SECOND, n) for n in range(chunks)]

    def prepare(t, n):
        if t == GATED:
            loads[2 * n].wait()
            loads[2 * n + 1].wait()
            make_gated(n)
        elif t == FIRST:
            if n == 0:
                load_f1.wait()
            make_product(f1, xv, send1, n)
        elif t == BACK:
            if n == 0:
                arrange_factors()
            whole(GATED, n).wait_recv()
            make_product(f2pt, recv0, send2, n)
        else:
            whole(FIRST, n).wait_recv()
            make_product(f2p, recv1, send3, n)

    for u, (t, n) in enumerate(units):
        prepare(t, n)
        if u == 0:
            pl.semaphore_wait(barrier, count - 1 + ndp - 1)
        if u >= DEPTH:
            whole(*units[u - DEPTH]).wait_send()
        send(t, n)

    for n in range(chunks):
        whole(BACK, n).wait_recv()
    grad_one_part()
    dp_send(0)
    grad_two_part()
    dp_send(1)
    for n in range(chunks):
        make_product(f1t, recv2, spread, n)
    outs = [dp_finish(0, g1, g1_hbm), dp_finish(1, g2, g2_hbm)]

    for n in range(chunks):
        whole(SECOND, n).wait_recv()

        def tile(t, n=n):
            s = rowsof(t)
            monarch = recv3[n, s, :].astype(F32)
            send0[n, s, :] = (xv[n, s, :].astype(F32) * monarch).astype(BF16)
            send1[n, s, :] = (cv[n, s, :].astype(F32) * monarch + spread[n, s, :]).astype(BF16)

        loop(tiles, tile)
        cols = pl.ds(n * width, width)
        for i, (src, dst) in enumerate(((send0, mixed_hbm), (send1, gin_hbm))):
            copy = pltpu.make_async_copy(src.at[n], dst.at[:, cols], outsem.at[2 * n + i])
            copy.start()
            outs.append(copy)

    for t, n in units[len(units) - DEPTH :]:
        whole(t, n).wait_send()
    dp_whole(0).wait_send()
    dp_whole(1).wait_send()
    for copy in outs:
        copy.wait()


def local(inputs, cotangent, factor_one, factor_two):
    _, block, width = inputs.shape
    count = lax.axis_size("seq")
    ndp = lax.axis_size("dp")
    piece = block // ndp
    cut = width // CHUNKS
    chunked = pltpu.VMEM((CHUNKS, block, cut), BF16)
    square = pltpu.VMEM((block, block), BF16)
    spec = pl.BlockSpec(memory_space=pl.ANY)
    mixed, grad_input, grad_one, grad_two = pl.pallas_call(
        functools.partial(kernel, count, ndp),
        out_shape=(
            jax.ShapeDtypeStruct((block, width), BF16),
            jax.ShapeDtypeStruct((block, width), BF16),
            jax.ShapeDtypeStruct((piece, block), F32),
            jax.ShapeDtypeStruct((piece, block), F32),
        ),
        in_specs=[spec] * 4,
        out_specs=[spec] * 4,
        scratch_shapes=[chunked] * 2
        + [square] * 6
        + [chunked] * 8
        + [pltpu.VMEM((CHUNKS, block, cut), F32)]
        + [square] * 4
        + [pltpu.VMEM((piece, block), F32)] * 2
        + [
            pltpu.SemaphoreType.DMA((4, CHUNKS)),
            pltpu.SemaphoreType.DMA((4, CHUNKS)),
            pltpu.SemaphoreType.DMA((2,)),
            pltpu.SemaphoreType.DMA((2,)),
            pltpu.SemaphoreType.DMA((2 * CHUNKS + 2,)),
            pltpu.SemaphoreType.DMA((2 * CHUNKS + 2,)),
        ],
        compiler_params=pltpu.CompilerParams(
            collective_id=0, has_side_effects=True, vmem_limit_bytes=60 * 1024 * 1024
        ),
        cost_estimate=pl.CostEstimate(
            flops=12 * block * block * width, bytes_accessed=24 * block * width, transcendentals=0
        ),
    )(inputs[0], cotangent[0], factor_one[0], factor_two[0])
    return mixed[None], grad_input[None], grad_one[None], grad_two[None]


def solution(mesh):
    in_specs = (
        P("dp", "seq", None),
        P("dp", "seq", None),
        P("seq", None, None),
        P("seq", None, None),
    )
    out_specs = (
        P("dp", "seq", None),
        P("dp", "seq", None),
        P("seq", "dp", None),
        P("seq", "dp", None),
    )
    return jax.shard_map(local, mesh=mesh, in_specs=in_specs, out_specs=out_specs, check_vma=False)
```

```python
import functools

import jax
import jax.numpy as jnp
from jax import lax
from jax.experimental import pallas as pl
from jax.experimental.pallas import tpu as pltpu
from jax.sharding import PartitionSpec as P

MESH = pl.DeviceIdType.MESH
F32 = jnp.float32
BF16 = jnp.bfloat16

CHUNKS = 4
TILE = 256
DEPTH = 3

GATED, FIRST, BACK, SECOND = range(4)


def nn(a, b):
    return jnp.dot(a, b, preferred_element_type=F32)


def nt(a, b):
    return lax.dot_general(a, b, (((1,), (1,)), ((), ())), preferred_element_type=F32)


def loop(n, body):
    def step(i, carry):
        body(i)
        return carry

    lax.fori_loop(0, n, step, 0)


def kernel(
    count,
    ndp,
    x_hbm,
    c_hbm,
    f1_hbm,
    f2_hbm,
    mixed_hbm,
    gin_hbm,
    g1_hbm,
    g2_hbm,
    xv,
    cv,
    f1,
    f1t,
    f2,
    f2p,
    f2pt,
    tmp,
    send0,
    send1,
    send2,
    send3,
    recv0,
    recv1,
    recv2,
    recv3,
    spread,
    p1,
    p2,
    r1,
    r2,
    g1,
    g2,
    ssem,
    rsem,
    dssem,
    drsem,
    insem,
    outsem,
):
    sends = (send0, send1, send2, send3)
    recvs = (recv0, recv1, recv2, recv3)
    parts = (p1, p2)
    others = (r1, r2)
    chunks, block, width = xv.shape
    tiles = block // TILE
    rows = block // count
    piece = block // ndp
    dp = lax.axis_index("dp")
    me = lax.axis_index("seq")

    def rowsof(t):
        return pl.ds(pl.multiple_of(t * TILE, TILE), TILE)

    def load(src, dst, i):
        return pltpu.make_async_copy(src, dst, insem.at[i])

    loads = []
    for n in range(chunks):
        cols = pl.ds(n * width, width)
        loads.append(load(x_hbm.at[:, cols], xv.at[n], 2 * n))
        loads.append(load(c_hbm.at[:, cols], cv.at[n], 2 * n + 1))
    load_f1 = load(f1_hbm, f1, 2 * chunks)
    load_f2 = load(f2_hbm, f2, 2 * chunks + 1)
    for copy in loads[:2]:
        copy.start()

    barrier = pltpu.get_barrier_semaphore()

    def greet_seq(i):
        pl.semaphore_signal(
            barrier, inc=1, device_id=(dp, (me + 1 + i) % count), device_id_type=MESH
        )

    def greet_dp(i):
        pl.semaphore_signal(
            barrier, inc=1, device_id=((dp + 1 + i) % ndp, me), device_id_type=MESH
        )

    loop(count - 1, greet_seq)
    loop(ndp - 1, greet_dp)
    for copy in loads[2:]:
        copy.start()
    load_f1.start()
    load_f2.start()

    def seq_copy(t, n, source, target, size, to):
        return pltpu.make_async_remote_copy(
            src_ref=sends[t].at[n, pl.ds(source, size)],
            dst_ref=recvs[t].at[n, pl.ds(target, size)],
            send_sem=ssem.at[t, n],
            recv_sem=rsem.at[t, n],
            device_id=(dp, to),
            device_id_type=MESH,
        )

    mine = pl.multiple_of(me * rows, rows)

    def send(t, n):
        def one(i):
            j = i // 2
            far = count // 2 + ((j + 1) // 2) * (2 * (j % 2) - 1)
            near = (1 - j % 2) * (1 + j // 2) + (j % 2) * (count - 1 - j // 2)
            to = (me + (1 - i % 2) * far + (i % 2) * near) % count
            seq_copy(t, n, pl.multiple_of(to * rows, rows), mine, rows, to).start()

        loop(count - 1, one)
        recvs[t][n, pl.ds(mine, rows), :] = sends[t][n, pl.ds(mine, rows), :]

    def whole(t, n):
        return seq_copy(t, n, 0, 0, (count - 1) * rows, (me + 1) % count)

    def dp_copy(g, source, target, size, to):
        return pltpu.make_async_remote_copy(
            src_ref=parts[g].at[pl.ds(source, size)],
            dst_ref=others[g].at[pl.ds(target, size)],
            send_sem=dssem.at[g],
            recv_sem=drsem.at[g],
            device_id=(to, me),
            device_id_type=MESH,
        )

    own = pl.multiple_of(dp * piece, piece)

    def dp_send(g):
        def one(i):
            to = (dp + 1 + i) % ndp
            dp_copy(g, pl.multiple_of(to * piece, piece), own, piece, to).start()

        loop(ndp - 1, one)

    def dp_whole(g):
        return dp_copy(g, 0, 0, (ndp - 1) * piece, (dp + 1) % ndp)

    def dp_finish(g, out, out_hbm):
        dp_whole(g).wait_recv()
        others[g][pl.ds(own, piece), :] = parts[g][pl.ds(own, piece), :]
        step = min(piece, 128)

        def add(i):
            total = others[g][pl.ds(pl.multiple_of(i * step, step), step), :].astype(F32)
            for d in range(1, ndp):
                at = pl.multiple_of(d * piece + i * step, step)
                total += others[g][pl.ds(at, step), :].astype(F32)
            out[pl.ds(pl.multiple_of(i * step, step), step), :] = total

        loop(piece // step, add)
        copy = pltpu.make_async_copy(out, out_hbm, outsem.at[2 * chunks + g])
        copy.start()
        return copy

    shift = count.bit_length() - 1
    back_shift = rows.bit_length() - 1

    def select(t, forth):
        row = lax.broadcasted_iota(jnp.int32, (TILE, block), 0) + t * TILE
        col = lax.broadcasted_iota(jnp.int32, (TILE, block), 1)
        if forth:
            want = (row & (rows - 1)) * count + lax.shift_right_logical(
                row, jnp.full_like(row, back_shift)
            )
        else:
            want = (row & (count - 1)) * rows + lax.shift_right_logical(
                row, jnp.full_like(row, shift)
            )
        return jnp.where(col == want, 1.0, 0.0).astype(BF16)

    def identity(t):
        row = lax.broadcasted_iota(jnp.int32, (TILE, block), 0) + t * TILE
        col = lax.broadcasted_iota(jnp.int32, (TILE, block), 1)
        return jnp.where(col == row, 1.0, 0.0).astype(BF16)

    def make_gated(n):
        def tile(t):
            s = rowsof(t)
            send0[n, s, :] = (cv[n, s, :].astype(F32) * xv[n, s, :].astype(F32)).astype(BF16)

        loop(tiles, tile)

    def make_product(left, right, out, n):
        def tile(t):
            s = rowsof(t)
            out[n, s, :] = nn(left[s, :], right[n]).astype(out.dtype)

        loop(tiles, tile)

    def arrange_factors():
        def flip(t):
            f1t[rowsof(t), :] = nt(identity(t), f1[...]).astype(BF16)

        loop(tiles, flip)

        load_f2.wait()

        def one(t):
            tmp[rowsof(t), :] = nn(select(t, True), f2[...]).astype(BF16)

        def two(t):
            f2pt[rowsof(t), :] = nt(select(t, True), tmp[...]).astype(BF16)

        def three(t):
            tmp[rowsof(t), :] = nt(select(t, True), f2[...]).astype(BF16)

        def four(t):
            f2p[rowsof(t), :] = nt(select(t, True), tmp[...]).astype(BF16)

        loop(tiles, one)
        loop(tiles, two)
        loop(tiles, three)
        loop(tiles, four)

    def grad_two_part():
        def outer(t):
            s = rowsof(t)
            total = nt(recv0[0, s, :], recv1[0])
            for n in range(1, chunks):
                total += nt(recv0[n, s, :], recv1[n])
            p2[s, :] = total.astype(BF16)

        def one(t):
            tmp[rowsof(t), :] = nt(select(t, False), p2[...]).astype(BF16)

        def two(t):
            p2[rowsof(t), :] = nt(select(t, False), tmp[...]).astype(BF16)

        loop(tiles, outer)
        loop(tiles, one)
        loop(tiles, two)

    def grad_one_part():
        def outer(t):
            s = rowsof(t)
            total = nt(recv2[0, s, :], xv[0])
            for n in range(1, chunks):
                total += nt(recv2[n, s, :], xv[n])
            p1[s, :] = total.astype(BF16)

        loop(tiles, outer)

    units = [(t, n) for t in (GATED, FIRST, BACK, SECOND) for n in range(chunks)]
    seen = set()

    def arrived(t, n):
        if (t, n) not in seen:
            seen.add((t, n))
            whole(t, n).wait_recv()

    def prepare(t, n):
        if t == GATED:
            loads[2 * n].wait()
            loads[2 * n + 1].wait()
            make_gated(n)
        elif t == FIRST:
            make_product(f1, xv, send1, n)
        elif t == BACK:
            arrived(GATED, n)
            make_product(f2pt, recv0, send2, n)
        else:
            arrived(FIRST, n)
            make_product(f2p, recv1, send3, n)

    for u, (t, n) in enumerate(units):
        prepare(t, n)
        if u == 0:
            pl.semaphore_wait(barrier, count - 1 + ndp - 1)
        if u >= DEPTH:
            whole(*units[u - DEPTH]).wait_send()
        send(t, n)
        if u == DEPTH - 1:
            load_f1.wait()
            arrange_factors()
        if u == 2 * chunks + DEPTH - 1:
            for i in range(chunks):
                arrived(GATED, i)
                arrived(FIRST, i)
            grad_two_part()
            dp_send(1)
        if u == 3 * chunks + DEPTH - 1:
            for i in range(chunks):
                arrived(BACK, i)
            grad_one_part()
            dp_send(0)

    for n in range(chunks):
        make_product(f1t, recv2, spread, n)
    outs = [dp_finish(1, g2, g2_hbm)]

    for n in range(chunks):
        if n == chunks - 1:
            outs.append(dp_finish(0, g1, g1_hbm))
        arrived(SECOND, n)

        def tile(t, n=n):
            s = rowsof(t)
            monarch = recv3[n, s, :].astype(F32)
            send0[n, s, :] = (xv[n, s, :].astype(F32) * monarch).astype(BF16)
            send1[n, s, :] = (cv[n, s, :].astype(F32) * monarch + spread[n, s, :]).astype(BF16)

        loop(tiles, tile)
        cols = pl.ds(n * width, width)
        for i, (src, dst) in enumerate(((send0, mixed_hbm), (send1, gin_hbm))):
            copy = pltpu.make_async_copy(src.at[n], dst.at[:, cols], outsem.at[2 * n + i])
            copy.start()
            outs.append(copy)

    for t, n in units[len(units) - DEPTH :]:
        whole(t, n).wait_send()
    dp_whole(0).wait_send()
    dp_whole(1).wait_send()
    for copy in outs:
        copy.wait()


def copy_out(*refs):
    half = len(refs) // 2
    for src, dst in zip(refs[:half], refs[half:]):
        dst[...] = src[...]


def hand_over(arrays):
    steps = 4
    specs = [pl.BlockSpec((a.shape[0] // steps, a.shape[1]), lambda i: (i, 0)) for a in arrays]
    return pl.pallas_call(
        copy_out,
        grid=(steps,),
        in_specs=specs,
        out_specs=specs,
        out_shape=[jax.ShapeDtypeStruct(a.shape, a.dtype) for a in arrays],
        compiler_params=pltpu.CompilerParams(vmem_limit_bytes=60 * 1024 * 1024),
    )(*arrays)


def local(inputs, cotangent, factor_one, factor_two):
    _, block, width = inputs.shape
    count = lax.axis_size("seq")
    ndp = lax.axis_size("dp")
    piece = block // ndp
    cut = width // CHUNKS
    chunked = pltpu.VMEM((CHUNKS, block, cut), BF16)
    square = pltpu.VMEM((block, block), BF16)
    spec = pl.BlockSpec(memory_space=pl.ANY)
    results = pl.pallas_call(
        functools.partial(kernel, count, ndp),
        out_shape=(
            jax.ShapeDtypeStruct((block, width), BF16),
            jax.ShapeDtypeStruct((block, width), BF16),
            jax.ShapeDtypeStruct((piece, block), F32),
            jax.ShapeDtypeStruct((piece, block), F32),
        ),
        in_specs=[spec] * 4,
        out_specs=[spec] * 4,
        scratch_shapes=[chunked] * 2
        + [square] * 6
        + [chunked] * 8
        + [pltpu.VMEM((CHUNKS, block, cut), F32)]
        + [square] * 4
        + [pltpu.VMEM((piece, block), F32)] * 2
        + [
            pltpu.SemaphoreType.DMA((4, CHUNKS)),
            pltpu.SemaphoreType.DMA((4, CHUNKS)),
            pltpu.SemaphoreType.DMA((2,)),
            pltpu.SemaphoreType.DMA((2,)),
            pltpu.SemaphoreType.DMA((2 * CHUNKS + 2,)),
            pltpu.SemaphoreType.DMA((2 * CHUNKS + 2,)),
        ],
        compiler_params=pltpu.CompilerParams(
            collective_id=0, has_side_effects=True, vmem_limit_bytes=60 * 1024 * 1024
        ),
        cost_estimate=pl.CostEstimate(
            flops=12 * block * block * width, bytes_accessed=24 * block * width, transcendentals=0
        ),
    )(inputs[0], cotangent[0], factor_one[0], factor_two[0])
    return tuple(a[None] for a in hand_over(results))


def solution(mesh):
    in_specs = (
        P("dp", "seq", None),
        P("dp", "seq", None),
        P("seq", None, None),
        P("seq", None, None),
    )
    out_specs = (
        P("dp", "seq", None),
        P("dp", "seq", None),
        P("seq", "dp", None),
        P("seq", "dp", None),
    )
    return jax.shard_map(local, mesh=mesh, in_specs=in_specs, out_specs=out_specs, check_vma=False)
```

```python
import functools

import jax
import jax.numpy as jnp
from jax import lax
from jax.experimental import pallas as pl
from jax.experimental.pallas import tpu as pltpu
from jax.sharding import PartitionSpec as P

MESH = pl.DeviceIdType.MESH
F32 = jnp.float32
BF16 = jnp.bfloat16

CHUNKS = 4
TILE = 256
DEPTH = 3

GATED, FIRST, BACK, SECOND = range(4)


def nn(a, b):
    return jnp.dot(a, b, preferred_element_type=F32)


def nt(a, b):
    return lax.dot_general(a, b, (((1,), (1,)), ((), ())), preferred_element_type=F32)


def loop(n, body):
    def step(i, carry):
        body(i)
        return carry

    lax.fori_loop(0, n, step, 0)


def kernel(
    count,
    ndp,
    x_hbm,
    c_hbm,
    f1_hbm,
    f2_hbm,
    mixed,
    gin,
    g1,
    g2,
    xv,
    cv,
    f1,
    f1t,
    f2,
    f2p,
    f2pt,
    tmp,
    send0,
    send1,
    send2,
    send3,
    recv0,
    recv1,
    recv2,
    recv3,
    spread,
    p1,
    p2,
    r1,
    r2,
    ssem,
    rsem,
    dssem,
    drsem,
    insem,
):
    sends = (send0, send1, send2, send3)
    recvs = (recv0, recv1, recv2, recv3)
    parts = (p1, p2)
    others = (r1, r2)
    chunks, block, width = xv.shape
    tiles = block // TILE
    rows = block // count
    piece = block // ndp
    dp = lax.axis_index("dp")
    me = lax.axis_index("seq")

    def rowsof(t):
        return pl.ds(pl.multiple_of(t * TILE, TILE), TILE)

    def load(src, dst, i):
        return pltpu.make_async_copy(src, dst, insem.at[i])

    loads = []
    for n in range(chunks):
        cols = pl.ds(n * width, width)
        loads.append(load(x_hbm.at[:, cols], xv.at[n], 2 * n))
        loads.append(load(c_hbm.at[:, cols], cv.at[n], 2 * n + 1))
    load_f1 = load(f1_hbm, f1, 2 * chunks)
    load_f2 = load(f2_hbm, f2, 2 * chunks + 1)
    for copy in loads[:2]:
        copy.start()

    barrier = pltpu.get_barrier_semaphore()

    def greet_seq(i):
        pl.semaphore_signal(
            barrier, inc=1, device_id=(dp, (me + 1 + i) % count), device_id_type=MESH
        )

    def greet_dp(i):
        pl.semaphore_signal(
            barrier, inc=1, device_id=((dp + 1 + i) % ndp, me), device_id_type=MESH
        )

    loop(count - 1, greet_seq)
    loop(ndp - 1, greet_dp)
    for copy in loads[2:]:
        copy.start()
    load_f1.start()
    load_f2.start()

    def seq_copy(t, n, source, target, size, to):
        return pltpu.make_async_remote_copy(
            src_ref=sends[t].at[n, pl.ds(source, size)],
            dst_ref=recvs[t].at[n, pl.ds(target, size)],
            send_sem=ssem.at[t, n],
            recv_sem=rsem.at[t, n],
            device_id=(dp, to),
            device_id_type=MESH,
        )

    mine = pl.multiple_of(me * rows, rows)

    def send(t, n):
        def one(i):
            j = i // 2
            far = count // 2 + ((j + 1) // 2) * (2 * (j % 2) - 1)
            near = (1 - j % 2) * (1 + j // 2) + (j % 2) * (count - 1 - j // 2)
            to = (me + (1 - i % 2) * far + (i % 2) * near) % count
            seq_copy(t, n, pl.multiple_of(to * rows, rows), mine, rows, to).start()

        loop(count - 1, one)
        recvs[t][n, pl.ds(mine, rows), :] = sends[t][n, pl.ds(mine, rows), :]

    def whole(t, n):
        return seq_copy(t, n, 0, 0, (count - 1) * rows, (me + 1) % count)

    def dp_copy(g, source, target, size, to):
        return pltpu.make_async_remote_copy(
            src_ref=parts[g].at[pl.ds(source, size)],
            dst_ref=others[g].at[pl.ds(target, size)],
            send_sem=dssem.at[g],
            recv_sem=drsem.at[g],
            device_id=(to, me),
            device_id_type=MESH,
        )

    own = pl.multiple_of(dp * piece, piece)

    def dp_send(g):
        def one(i):
            to = (dp + 1 + i) % ndp
            dp_copy(g, pl.multiple_of(to * piece, piece), own, piece, to).start()

        loop(ndp - 1, one)

    def dp_whole(g):
        return dp_copy(g, 0, 0, (ndp - 1) * piece, (dp + 1) % ndp)

    def dp_finish(g, out):
        dp_whole(g).wait_recv()
        others[g][pl.ds(own, piece), :] = parts[g][pl.ds(own, piece), :]
        step = min(piece, 128)

        def add(i):
            total = others[g][pl.ds(pl.multiple_of(i * step, step), step), :].astype(F32)
            for d in range(1, ndp):
                at = pl.multiple_of(d * piece + i * step, step)
                total += others[g][pl.ds(at, step), :].astype(F32)
            out[pl.ds(pl.multiple_of(i * step, step), step), :] = total

        loop(piece // step, add)

    shift = count.bit_length() - 1
    back_shift = rows.bit_length() - 1

    def select(t, forth):
        row = lax.broadcasted_iota(jnp.int32, (TILE, block), 0) + t * TILE
        col = lax.broadcasted_iota(jnp.int32, (TILE, block), 1)
        if forth:
            want = (row & (rows - 1)) * count + lax.shift_right_logical(
                row, jnp.full_like(row, back_shift)
            )
        else:
            want = (row & (count - 1)) * rows + lax.shift_right_logical(
                row, jnp.full_like(row, shift)
            )
        return jnp.where(col == want, 1.0, 0.0).astype(BF16)

    def identity(t):
        row = lax.broadcasted_iota(jnp.int32, (TILE, block), 0) + t * TILE
        col = lax.broadcasted_iota(jnp.int32, (TILE, block), 1)
        return jnp.where(col == row, 1.0, 0.0).astype(BF16)

    def make_gated(n):
        def tile(t):
            s = rowsof(t)
            send0[n, s, :] = (cv[n, s, :].astype(F32) * xv[n, s, :].astype(F32)).astype(BF16)

        loop(tiles, tile)

    def make_product(left, right, out, n):
        def tile(t):
            s = rowsof(t)
            out[n, s, :] = nn(left[s, :], right[n]).astype(out.dtype)

        loop(tiles, tile)

    def arrange_factors():
        def flip(t):
            f1t[rowsof(t), :] = nt(identity(t), f1[...]).astype(BF16)

        loop(tiles, flip)

        load_f2.wait()

        def one(t):
            tmp[rowsof(t), :] = nn(select(t, True), f2[...]).astype(BF16)

        def two(t):
            f2pt[rowsof(t), :] = nt(select(t, True), tmp[...]).astype(BF16)

        def three(t):
            tmp[rowsof(t), :] = nt(select(t, True), f2[...]).astype(BF16)

        def four(t):
            f2p[rowsof(t), :] = nt(select(t, True), tmp[...]).astype(BF16)

        loop(tiles, one)
        loop(tiles, two)
        loop(tiles, three)
        loop(tiles, four)

    def grad_two_part():
        def outer(t):
            s = rowsof(t)
            total = nt(recv0[0, s, :], recv1[0])
            for n in range(1, chunks):
                total += nt(recv0[n, s, :], recv1[n])
            p2[s, :] = total.astype(BF16)

        def one(t):
            tmp[rowsof(t), :] = nt(select(t, False), p2[...]).astype(BF16)

        def two(t):
            p2[rowsof(t), :] = nt(select(t, False), tmp[...]).astype(BF16)

        loop(tiles, outer)
        loop(tiles, one)
        loop(tiles, two)

    def grad_one_part():
        def outer(t):
            s = rowsof(t)
            total = nt(recv2[0, s, :], xv[0])
            for n in range(1, chunks):
                total += nt(recv2[n, s, :], xv[n])
            p1[s, :] = total.astype(BF16)

        loop(tiles, outer)

    units = [(t, n) for t in (GATED, FIRST, BACK, SECOND) for n in range(chunks)]
    seen = set()

    def arrived(t, n):
        if (t, n) not in seen:
            seen.add((t, n))
            whole(t, n).wait_recv()

    def prepare(t, n):
        if t == GATED:
            loads[2 * n].wait()
            loads[2 * n + 1].wait()
            make_gated(n)
        elif t == FIRST:
            make_product(f1, xv, send1, n)
        elif t == BACK:
            arrived(GATED, n)
            make_product(f2pt, recv0, send2, n)
        else:
            arrived(FIRST, n)
            make_product(f2p, recv1, send3, n)

    for u, (t, n) in enumerate(units):
        prepare(t, n)
        if u == 0:
            pl.semaphore_wait(barrier, count - 1 + ndp - 1)
        if u >= DEPTH:
            whole(*units[u - DEPTH]).wait_send()
        send(t, n)
        if u == DEPTH - 1:
            load_f1.wait()
            arrange_factors()
        if u == 2 * chunks + DEPTH - 1:
            for i in range(chunks):
                arrived(GATED, i)
                arrived(FIRST, i)
            grad_two_part()
            dp_send(1)
        if u == 3 * chunks + DEPTH - 1:
            for i in range(chunks):
                arrived(BACK, i)
            grad_one_part()
            dp_send(0)

    for n in range(chunks):
        make_product(f1t, recv2, spread, n)
    dp_finish(1, g2)

    for n in range(chunks):
        if n == chunks - 1:
            dp_finish(0, g1)
        arrived(SECOND, n)

        cols = pl.ds(n * width, width)

        def tile(t, n=n, cols=cols):
            s = rowsof(t)
            monarch = recv3[n, s, :].astype(F32)
            mixed[s, cols] = (xv[n, s, :].astype(F32) * monarch).astype(BF16)
            gin[s, cols] = (cv[n, s, :].astype(F32) * monarch + spread[n, s, :]).astype(BF16)

        loop(tiles, tile)

    for t, n in units[len(units) - DEPTH :]:
        whole(t, n).wait_send()
    dp_whole(0).wait_send()
    dp_whole(1).wait_send()


def copy_out(*refs):
    half = len(refs) // 2
    sem = refs[-1]
    copies = [
        pltpu.make_async_copy(src, dst, sem.at[i])
        for i, (src, dst) in enumerate(zip(refs[:half], refs[half:-1]))
    ]
    for copy in copies:
        copy.start()
    for copy in copies:
        copy.wait()


def hand_over(arrays):
    return pl.pallas_call(
        copy_out,
        in_specs=[pl.BlockSpec(memory_space=pltpu.VMEM)] * len(arrays),
        out_specs=[pl.BlockSpec(memory_space=pl.ANY)] * len(arrays),
        out_shape=[jax.ShapeDtypeStruct(a.shape, a.dtype) for a in arrays],
        scratch_shapes=[pltpu.SemaphoreType.DMA((len(arrays),))],
    )(*arrays)


def local(inputs, cotangent, factor_one, factor_two):
    _, block, width = inputs.shape
    count = lax.axis_size("seq")
    ndp = lax.axis_size("dp")
    piece = block // ndp
    cut = width // CHUNKS
    chunked = pltpu.VMEM((CHUNKS, block, cut), BF16)
    square = pltpu.VMEM((block, block), BF16)
    spec = pl.BlockSpec(memory_space=pl.ANY)
    results = pl.pallas_call(
        functools.partial(kernel, count, ndp),
        out_shape=(
            pltpu.VMEM((block, width), BF16),
            pltpu.VMEM((block, width), BF16),
            pltpu.VMEM((piece, block), F32),
            pltpu.VMEM((piece, block), F32),
        ),
        in_specs=[spec] * 4,
        out_specs=[pl.BlockSpec(memory_space=pltpu.VMEM)] * 4,
        scratch_shapes=[chunked] * 2
        + [square] * 6
        + [chunked] * 8
        + [pltpu.VMEM((CHUNKS, block, cut), F32)]
        + [square] * 4
        + [
            pltpu.SemaphoreType.DMA((4, CHUNKS)),
            pltpu.SemaphoreType.DMA((4, CHUNKS)),
            pltpu.SemaphoreType.DMA((2,)),
            pltpu.SemaphoreType.DMA((2,)),
            pltpu.SemaphoreType.DMA((2 * CHUNKS + 2,)),
        ],
        compiler_params=pltpu.CompilerParams(
            collective_id=0, has_side_effects=True, vmem_limit_bytes=54 * 1024 * 1024
        ),
        cost_estimate=pl.CostEstimate(
            flops=12 * block * block * width, bytes_accessed=24 * block * width, transcendentals=0
        ),
    )(inputs[0], cotangent[0], factor_one[0], factor_two[0])
    return tuple(a[None] for a in hand_over(results))


def solution(mesh):
    in_specs = (
        P("dp", "seq", None),
        P("dp", "seq", None),
        P("seq", None, None),
        P("seq", None, None),
    )
    out_specs = (
        P("dp", "seq", None),
        P("dp", "seq", None),
        P("seq", "dp", None),
        P("seq", "dp", None),
    )
    return jax.shard_map(local, mesh=mesh, in_specs=in_specs, out_specs=out_specs, check_vma=False)
```
